512 devices in a mesh: row: 32 (over y, z_hi, core), col: 16 (over x, z_lo).
Axes of the slice: x: 4, y: 4, z: 16 (z_hi: 4, z_lo: 4; z = z_hi * 4 + z_lo), core: 2. Of those that a mesh axis runs over, the one named last changes fastest.
Arguments:
- tokens: bfloat16 [4096, 6144], P('row', 'col'), may hold values from -6 to 6
- ln_gain: float32 [6144], P('col'), may hold values from 0.1 to 1.9
- qkv_weight: bfloat16 [6144, 32, 384], P('col', 'row'), may hold values from -0.078125 to 0.078125
- q_gain: float32 [32, 128], P('row'), may hold values from 0.6 to 1.6
- k_gain: float32 [32, 128], P('row'), may hold values from 0.6 to 1.6
Outputs:
- attended: float32 [4096, 32, 128], P('col', 'row')
The draws below stay inside these ranges and needn't reach their ends.
All inputs are finite; a program needn't handle non-finite values.
Results may differ from the reference program's by a relative error of at most 0.04.
Values may be sent and summed in bfloat16 or wider, within the bound.
No kernel may reach another device: no remote copies, remote signals or barrier semaphores. Data moves between devices by JAX's collectives and lax.ppermute only.
A program may use at most 64 MiB of HBM per device.

```python
import math
import jax
import jax.numpy as jnp
from jax import lax

D = 6144
HS = 128
HEADS = 32
TOKENS = 4096
N_COL = 16


def shard_levels(own_key, shape, shards, low, high):
    loudness = 1.0
    for axis_at, shards_of in shards:
        draws = jax.random.uniform(jax.random.fold_in(jax.random.fold_in(own_key, 6), axis_at), (shards_of,), jnp.float32, low / len(shards), high / len(shards))
        loudness = loudness * jnp.repeat(jnp.exp(draws), shape[axis_at] // shards_of).reshape((-1,) + (1,) * (len(shape) - 1 - axis_at))
    return loudness


def noise(stream_key, dims, width, limit, cuts=(), dtype=jnp.bfloat16):
    array = width * jax.random.normal(stream_key, dims, jnp.float32)
    if cuts:
        array = array * shard_levels(stream_key, dims, cuts, -0.22, 0.18)
    return jnp.clip(array, -limit, limit).astype(dtype)


def setup_inputs(seed: int = 0) -> dict:
    splits = jax.random.split(jax.random.key(seed), 6)
    return {
        "tokens": noise(splits[0], (TOKENS, D), 1.0, 6.0, ((0, 32), (1, 16))),
        "ln_gain": jnp.clip(1.0 + 0.18 * jax.random.normal(splits[1], (D,), jnp.float32), 0.1, 1.9),
        "qkv_weight": noise(splits[2], (D, HEADS, 3 * HS), D ** -0.5, 0.078125, ((0, 16), (1, 32))),
        "q_gain": jnp.clip(jnp.exp(math.log(1.6) - 0.98082923 * jax.random.uniform(splits[3], (HEADS, HS), jnp.float32) ** shard_levels(splits[3], (HEADS, HS), ((0, 32),), -0.2, 0.2)), 0.6, 1.6),
        "k_gain": jnp.clip(jnp.exp(math.log(1.6) - 0.98082923 * jax.random.uniform(splits[4], (HEADS, HS), jnp.float32) ** shard_levels(splits[4], (HEADS, HS), ((0, 32),), -0.2, 0.2)), 0.6, 1.6),
    }


epsilon = 1e-06

def head_norm(vectors, gain):
    average = lax.optimization_barrier(jnp.mean(vectors, axis=-1, keepdims=True))
    centred = vectors - average
    variance = lax.optimization_barrier(jnp.mean(centred * centred, axis=-1, keepdims=True))
    return (centred * lax.rsqrt(variance + epsilon) * gain).astype(jnp.bfloat16)

def reference(tokens, ln_gain, qkv_weight, q_gain, k_gain):
    widened = tokens.astype(jnp.float32)
    average = lax.optimization_barrier(jnp.sum(widened, axis=1)) / D
    variance = lax.optimization_barrier(jnp.sum(widened * widened, axis=1)) / D - average * average
    normed = ((widened - average[:, None]) * lax.rsqrt(variance + epsilon)[:, None] * ln_gain).astype(jnp.bfloat16)
    width_dev = D // N_COL
    blocks = normed.reshape(TOKENS, N_COL, width_dev).transpose(1, 0, 2)
    weight_blocks = qkv_weight.reshape(N_COL, width_dev, HEADS * 3 * HS)

    def accumulate(running, operands):
        block, weight = operands
        partial_sum = jnp.dot(block, weight, preferred_element_type=jnp.float32).astype(jnp.bfloat16)
        partial_sum = lax.optimization_barrier(partial_sum)
        return (running + partial_sum.astype(jnp.float32), None)
    projected, unused = lax.scan(accumulate, jnp.zeros((TOKENS, HEADS * 3 * HS), jnp.float32), (blocks, weight_blocks))
    projected = projected.reshape(TOKENS, HEADS, 3, HS)
    queries = head_norm(projected[:, :, 0], q_gain)
    keys = head_norm(projected[:, :, 1], k_gain)
    values = projected[:, :, 2].astype(jnp.bfloat16)

    def one_head(operands):
        head_queries, head_keys, head_values = operands
        scores = jnp.dot(head_queries, head_keys.T, preferred_element_type=jnp.float32) * HS ** (-0.5)
        raised = jnp.exp(scores)
        weights = (raised / lax.optimization_barrier(jnp.sum(raised, axis=-1, keepdims=True))).astype(jnp.bfloat16)
        return jnp.dot(weights, head_values, preferred_element_type=jnp.float32)
    attended = lax.map(one_head, (queries.transpose(1, 0, 2), keys.transpose(1, 0, 2), values.transpose(1, 0, 2)))
    return attended.transpose(1, 0, 2)
```

```python
import jax
import jax.numpy as jnp
from jax import lax
from jax.experimental import pallas as pl
from jax.experimental.pallas import tpu as pltpu
from jax.sharding import Mesh, PartitionSpec as P

D = 6144
HS = 128
FB = 384
FD = 4 * FB
TB = 128
EXTRA = 16
EPS = 1e-06

bf16 = jnp.bfloat16
f32 = jnp.float32

AXES = ("y", "zh", "core", "x", "zl")


def pieces(v):
    a = v.astype(bf16)
    r = v - a.astype(f32)
    b = r.astype(bf16)
    c = (r - b.astype(f32)).astype(bf16)
    return a.astype(f32), b.astype(f32), c.astype(f32)


def shift(x, axis, k):
    return lax.ppermute(x, axis, [(i, (i + k) % 4) for i in range(4)])


def call(kernel, out_shape, n_vmem, limit, flops, nbytes, trans=0, name=None):
    return pl.pallas_call(
        kernel,
        out_shape=out_shape,
        in_specs=[pl.BlockSpec(memory_space=pltpu.SMEM)] + [pl.BlockSpec(memory_space=pltpu.VMEM)] * n_vmem,
        out_specs=jax.tree.map(lambda _: pl.BlockSpec(memory_space=pltpu.VMEM), out_shape),
        compiler_params=pltpu.CompilerParams(vmem_limit_bytes=limit << 20),
        cost_estimate=pl.CostEstimate(flops=flops, bytes_accessed=nbytes, transcendentals=trans),
        name=name,
    )


def prep_kernel(s_ref, own_ref, oth_ref, w_ref, sums_ref):
    turn, core = s_ref[0], s_ref[1]
    for k in range(4):
        j = lax.rem(k + turn, 4)
        own, oth = own_ref[j], oth_ref[j]
        w_ref[k * FB : (k + 1) * FB, 0:FB] = jnp.where(core == 0, own, oth)
        w_ref[k * FB : (k + 1) * FB, FB : 2 * FB] = jnp.where(core == 0, oth, own)
    sums_ref[...] = jnp.dot(jnp.ones((8, FD), bf16), w_ref[...], preferred_element_type=f32)


def project_kernel(s_ref, x0, x1, x2, x3, w_ref, sums_ref, out_ref):
    y = s_ref[2]
    ones = jnp.ones((8, 128), f32)
    colsum = sums_ref[0:1, :]
    col_rows = jnp.concatenate(pieces(colsum), axis=0)
    for k, x_ref in enumerate((x0, x1, x2, x3)):
        x = x_ref[...]
        total = jnp.zeros((TB, 128), f32)
        squares = jnp.zeros((TB, 128), f32)
        for i in range(FD // 128):
            t = x[:, i * 128 : (i + 1) * 128].astype(f32)
            total = total + t
            squares = squares + t * t
        mean = jnp.sum(total, axis=1, keepdims=True) * (1.0 / FD)
        nt = (((1,), (1,)), ((), ()))
        s1 = lax.dot_general(ones, total, nt, precision=lax.Precision.HIGHEST, preferred_element_type=f32)
        s2 = lax.dot_general(ones, squares, nt, precision=lax.Precision.HIGHEST, preferred_element_type=f32)
        stats = jnp.concatenate(pieces(s1[0:1]) + pieces(s2[0:1]), axis=0)
        stats = jnp.concatenate([stats, jnp.zeros((6, FB - TB), f32)], axis=1)
        prod = jnp.dot(x, w_ref[...], preferred_element_type=f32) - mean * colsum
        at = lax.rem(y - k + 4, 4)
        for h in range(2):
            out_ref[h * 4 + at, 0:TB, :] = prod[:, h * FB : (h + 1) * FB].astype(bf16)
            out_ref[h * 4 + at, TB : TB + EXTRA, :] = jnp.concatenate(
                [stats, col_rows[:, h * FB : (h + 1) * FB], jnp.zeros((EXTRA - 9, FB), f32)], axis=0
            ).astype(bf16)


def norm_kernel(s_ref, r_ref, qg_ref, kg_ref, q_ref, kv_ref):
    for half in range(2):
        s1, s2, cs = [], [], []
        acc = jnp.zeros((TB, 3 * HS), f32)
        for x in range(4):
            blk = half * 4 + x
            acc = acc + r_ref[blk, 0:TB, :].astype(f32)
            e = r_ref[blk, TB : TB + EXTRA, :].astype(f32)
            s1.append(e[0:1, 0:TB] + e[1:2, 0:TB] + e[2:3, 0:TB])
            s2.append(e[3:4, 0:TB] + e[4:5, 0:TB] + e[5:6, 0:TB])
            cs.append(e[6:7] + e[7:8] + e[8:9])
        mean = (s1[0] + s1[1] + s1[2] + s1[3]) * (1.0 / D)
        var = (s2[0] + s2[1] + s2[2] + s2[3]) * (1.0 / D) - mean * mean
        rows = [s * (1.0 / FD) - mean for s in s1] + [lax.rsqrt(var + EPS)]
        cols = jnp.concatenate(rows + [jnp.zeros((TB - 5, TB), f32)], axis=0).T
        for x in range(4):
            acc = acc + cols[:, x : x + 1] * cs[x]
        proj = acc * cols[:, 4:5]

        def head_norm(v, gain):
            c = v - jnp.mean(v, axis=1, keepdims=True)
            return c * lax.rsqrt(jnp.mean(c * c, axis=1, keepdims=True) + EPS) * gain

        at = slice(half * TB, (half + 1) * TB)
        q_ref[at, :] = head_norm(proj[:, 0:HS], qg_ref[...]).astype(bf16)
        kv_ref[at, 0:HS] = head_norm(proj[:, HS : 2 * HS], kg_ref[...]).astype(bf16)
        kv_ref[at, HS : 2 * HS] = proj[:, 2 * HS : 3 * HS].astype(bf16)


def attend_kernel(s_ref, q0, q1, q2, q3, c0, c1, c2, c3, out_ref):
    zl = s_ref[3]
    kvs = (c0, c1, c2, c3)
    vts = [c[:, HS : 2 * HS].T for c in kvs]
    for j, q_ref in enumerate((q0, q1, q2, q3)):
        q = q_ref[...]
        n = q.shape[0]
        total = jnp.zeros((HS, n), f32)
        denom = jnp.zeros((1, n), f32)
        for c, vt in zip(kvs, vts):
            s = lax.dot_general(c[:, 0:HS], q, (((1,), (1,)), ((), ())), preferred_element_type=f32)
            p = jnp.exp(s * (HS ** -0.5))
            denom = denom + jnp.sum(p, axis=0, keepdims=True)
            total = total + jnp.dot(vt, p.astype(bf16), preferred_element_type=f32)
        at = lax.rem(zl - j + 4, 4)
        out_ref[at, 0:HS, :] = total.astype(bf16)
        out_ref[at, HS : HS + EXTRA, :] = jnp.concatenate(
            pieces(denom) + (jnp.zeros((EXTRA - 3, n), f32),), axis=0
        ).astype(bf16)


def combine_kernel(s_ref, r_ref, out_ref):
    total = jnp.zeros((HS, r_ref.shape[2]), f32)
    denom = jnp.zeros((1, r_ref.shape[2]), f32)
    for j in range(4):
        total = total + r_ref[j, 0:HS, :].astype(f32)
        e = r_ref[j, HS : HS + EXTRA, :].astype(f32)
        denom = denom + (e[0:1] + e[1:2] + e[2:3])
    out_ref[...] = (total / denom).T


def body(tokens, ln_gain, qkv_weight, q_gain, k_gain):
    y, zh, core, zl = (lax.axis_index(a).astype(jnp.int32) for a in ("y", "zh", "core", "zl"))
    where = jnp.stack([lax.rem(zl - zh + 4, 4), core, y, zl])

    parts = [
        lax.ppermute(tokens, ("zh", "zl"), [(a * 4 + b, ((b + k) % 4) * 4 + a) for a in range(4) for b in range(4)])
        for k in range(4)
    ]
    w = (ln_gain[:, None] * qkv_weight.reshape(FB, 3 * HS).astype(f32)).astype(bf16)
    own = jnp.stack([w] + [shift(w, "zl", k) for k in (1, 2, 3)])
    other = lax.ppermute(own, "core", [(0, 1), (1, 0)])
    weights, sums = call(
        prep_kernel,
        (jax.ShapeDtypeStruct((FD, 2 * FB), bf16), jax.ShapeDtypeStruct((8, 2 * FB), f32)),
        2, 24, 2 * 8 * FD * 2 * FB, 4 * FD * 2 * FB, name="prep",
    )(where, own, other)

    x0 = jnp.concatenate(parts, axis=1)
    xs = [x0] + [shift(x0, "y", k) for k in (1, 2, 3)]
    products = call(
        project_kernel,
        jax.ShapeDtypeStruct((8, TB + EXTRA, FB), bf16),
        6, 40, 2 * 4 * TB * FD * 2 * FB, 6 << 20, name="project",
    )(where, *xs, weights, sums)
    received = lax.all_to_all(products, ("core", "x"), split_axis=0, concat_axis=0, tiled=True)
    q, kv = call(
        norm_kernel,
        (jax.ShapeDtypeStruct((2 * TB, HS), bf16), jax.ShapeDtypeStruct((2 * TB, 2 * HS), bf16)),
        3, 24, 10 * 8 * TB * FB, 2 << 20, name="norm",
    )(where, received, q_gain, k_gain)

    qs = [q] + [shift(q, "zl", k) for k in (1, 2, 3)]
    kvs = [kv] + [shift(kv, "x", k) for k in (1, 2, 3)]
    partial = call(
        attend_kernel,
        jax.ShapeDtypeStruct((4, HS + EXTRA, 2 * TB), bf16),
        8, 40, 4 * 1024 * 1024 * HS, 2 << 20, 1 << 20, name="attend",
    )(where, *qs, *kvs)
    gathered = lax.all_to_all(partial, "zl", split_axis=0, concat_axis=0, tiled=True)
    out = call(
        combine_kernel,
        jax.ShapeDtypeStruct((2 * TB, HS), f32),
        1, 16, 8 * HS * 2 * TB, 1 << 20, name="combine",
    )(where, gathered)
    return out.reshape(2 * TB, 1, HS)


def solution(mesh):
    split = Mesh(mesh.devices.reshape(4, 4, 2, 4, 4), AXES)
    row, col = ("y", "zh", "core"), ("x", "zl")
    return jax.shard_map(
        body,
        mesh=split,
        in_specs=(P(row, col), P(col), P(col, row, None), P(row, None), P(row, None)),
        out_specs=P(col, row, None),
        check_vma=False,
    )
```

```python
import jax
import jax.numpy as jnp
from jax import lax
from jax.experimental import pallas as pl
from jax.experimental.pallas import tpu as pltpu
from jax.sharding import Mesh, PartitionSpec as P

D = 6144
HS = 128
FB = 384
FD = 4 * FB
TB = 128
QT = 32
EXTRA = 16
EPS = 1e-06

bf16 = jnp.bfloat16
f32 = jnp.float32

AXES = ("y", "zh", "core", "x", "zl")
GATHER = ("x",)
REDUCE = ("zl",)


def pieces(v):
    a = v.astype(bf16)
    r = v - a.astype(f32)
    b = r.astype(bf16)
    c = (r - b.astype(f32)).astype(bf16)
    return a.astype(f32), b.astype(f32), c.astype(f32)


def shift(x, axis, k):
    return lax.ppermute(x, axis, [(i, (i + k) % 4) for i in range(4)])


def swap(x, axis, k=1, n=2):
    return lax.ppermute(x, axis, [(i, i ^ k) for i in range(n)])


def call(kernel, out_shape, n_vmem, limit, flops, nbytes, trans=0, name=None, scratch=()):
    return pl.pallas_call(
        kernel,
        out_shape=out_shape,
        in_specs=[pl.BlockSpec(memory_space=pltpu.SMEM)] + [pl.BlockSpec(memory_space=pltpu.VMEM)] * n_vmem,
        scratch_shapes=scratch,
        out_specs=jax.tree.map(lambda _: pl.BlockSpec(memory_space=pltpu.VMEM), out_shape),
        compiler_params=pltpu.CompilerParams(vmem_limit_bytes=limit << 20),
        cost_estimate=pl.CostEstimate(flops=flops, bytes_accessed=nbytes, transcendentals=trans),
        name=name,
    )


def prep_kernel(s_ref, own_ref, oth_ref, w_ref, sums_ref):
    core = s_ref[0]
    for b in range(4):
        j = s_ref[4 + b]
        own, oth = own_ref[j], oth_ref[j]
        w_ref[b * FB : (b + 1) * FB, 0:FB] = jnp.where(core == 0, own, oth)
        w_ref[b * FB : (b + 1) * FB, FB : 2 * FB] = jnp.where(core == 0, oth, own)
    sums_ref[...] = jnp.dot(jnp.ones((8, FD), bf16), w_ref[...], preferred_element_type=f32)


def project_kernel(s_ref, x0, x2, x1, x3, w_ref, sums_ref, out_ref, xs_ref):
    for k, x_ref in ((0, x0), (2, x2), (1, x1), (3, x3)):
        block = lax.rem(s_ref[1] - k + 4, 4)
        to = pl.multiple_of(block * QT, QT)
        for a in range(4):
            for b in range(4):
                xs_ref[a, pl.ds(to, QT), b * FB : (b + 1) * FB] = x_ref[a * 4 + b]
    ones = jnp.ones((8, 128), f32)
    colsum = sums_ref[0:1, :]
    col_rows = jnp.concatenate(pieces(colsum), axis=0)
    for at in range(4):
        x = xs_ref[at]
        total = jnp.zeros((TB, 128), f32)
        squares = jnp.zeros((TB, 128), f32)
        for i in range(FD // 128):
            t = x[:, i * 128 : (i + 1) * 128].astype(f32)
            total = total + t
            squares = squares + t * t
        mean = jnp.sum(total, axis=1, keepdims=True) * (1.0 / FD)
        nt = (((1,), (1,)), ((), ()))
        s1 = lax.dot_general(ones, total, nt, precision=lax.Precision.HIGHEST, preferred_element_type=f32)
        s2 = lax.dot_general(ones, squares, nt, precision=lax.Precision.HIGHEST, preferred_element_type=f32)
        stats = jnp.concatenate(pieces(s1[0:1]) + pieces(s2[0:1]), axis=0)
        stats = jnp.concatenate([stats, jnp.zeros((6, FB - TB), f32)], axis=1)
        prod = jnp.dot(x, w_ref[...], preferred_element_type=f32) - mean * colsum
        for h in range(2):
            out_ref[h * 4 + at, 0:TB, :] = prod[:, h * FB : (h + 1) * FB].astype(bf16)
            out_ref[h * 4 + at, TB : TB + EXTRA, :] = jnp.concatenate(
                [stats, col_rows[:, h * FB : (h + 1) * FB], jnp.zeros((EXTRA - 9, FB), f32)], axis=0
            ).astype(bf16)


def norm_kernel(s_ref, r_ref, qg_ref, kg_ref, q_ref, kv_ref):
    for half in range(2):
        s1, s2, cs = [], [], []
        acc = jnp.zeros((TB, 3 * HS), f32)
        for x in range(4):
            blk = half * 4 + x
            acc = acc + r_ref[blk, 0:TB, :].astype(f32)
            e = r_ref[blk, TB : TB + EXTRA, :].astype(f32)
            s1.append(e[0:1, 0:TB] + e[1:2, 0:TB] + e[2:3, 0:TB])
            s2.append(e[3:4, 0:TB] + e[4:5, 0:TB] + e[5:6, 0:TB])
            cs.append(e[6:7] + e[7:8] + e[8:9])
        mean = (s1[0] + s1[1] + s1[2] + s1[3]) * (1.0 / D)
        var = (s2[0] + s2[1] + s2[2] + s2[3]) * (1.0 / D) - mean * mean
        rows = [s * (1.0 / FD) - mean for s in s1] + [lax.rsqrt(var + EPS)]
        cols = jnp.concatenate(rows + [jnp.zeros((TB - 5, TB), f32)], axis=0).T
        for x in range(4):
            acc = acc + cols[:, x : x + 1] * cs[x]
        proj = acc * cols[:, 4:5]

        def head_norm(v, gain):
            c = v - jnp.mean(v, axis=1, keepdims=True)
            return c * lax.rsqrt(jnp.mean(c * c, axis=1, keepdims=True) + EPS) * gain

        at = slice(half * TB, (half + 1) * TB)
        q_ref[at, :] = head_norm(proj[:, 0:HS], qg_ref[...]).astype(bf16)
        keys = head_norm(proj[:, HS : 2 * HS], kg_ref[...]).astype(bf16)
        values = proj[:, 2 * HS : 3 * HS].astype(bf16)
        for x in range(4):
            kv_ref[x, at, 0:HS] = keys
            kv_ref[x, at, HS : 2 * HS] = values


def attend_kernel(s_ref, q0, q1, q2, q3, kv_ref, out_ref, qs_ref):
    for k, q_ref in enumerate((q0, q1, q2, q3)):
        quarter = s_ref[4 + k]
        for a in range(4):
            for half in range(2):
                to = pl.multiple_of(half * TB + quarter * QT, QT)
                qs_ref[a, pl.ds(to, QT), :] = q_ref[half * TB + a * QT : half * TB + (a + 1) * QT, :]
    vts = [kv_ref[c, :, HS : 2 * HS].T for c in range(4)]
    for a in range(4):
        q = qs_ref[a]
        n = q.shape[0]
        total = jnp.zeros((HS, n), f32)
        denom = jnp.zeros((1, n), f32)
        for c in range(4):
            s = lax.dot_general(kv_ref[c, :, 0:HS], q, (((1,), (1,)), ((), ())), preferred_element_type=f32)
            p = jnp.exp(s * (HS ** -0.5))
            denom = denom + jnp.sum(p, axis=0, keepdims=True)
            total = total + jnp.dot(vts[c], p.astype(bf16), preferred_element_type=f32)
        out_ref[a, 0:HS, :] = total.astype(bf16)
        out_ref[a, HS : HS + EXTRA, :] = jnp.concatenate(
            pieces(denom) + (jnp.zeros((EXTRA - 3, n), f32),), axis=0
        ).astype(bf16)


def combine_kernel(s_ref, r_ref, out_ref):
    total = jnp.zeros((HS, r_ref.shape[2]), f32)
    denom = jnp.zeros((1, r_ref.shape[2]), f32)
    for j in range(4):
        total = total + r_ref[j, 0:HS, :].astype(f32)
        e = r_ref[j, HS : HS + EXTRA, :].astype(f32)
        denom = denom + (e[0:1] + e[1:2] + e[2:3])
    out_ref[...] = (total / denom).T


def body(tokens, ln_gain, qkv_weight, q_gain, k_gain):
    y, core, x = (lax.axis_index(a).astype(jnp.int32) for a in ("y", "core", "x"))
    where = jnp.stack([core, y, x, x] + [jnp.bitwise_xor(x, k) for k in range(4)])

    x0 = lax.all_to_all(
        jnp.concatenate([tokens] * 4, axis=0).reshape(16, QT, FB),
        ("zh",) + GATHER, split_axis=0, concat_axis=0, tiled=True,
    )
    w = (ln_gain[:, None] * qkv_weight.reshape(FB, 3 * HS).astype(f32)).astype(bf16)
    own = jnp.stack([w] + [swap(w, "x", k, 4) for k in (1, 2, 3)])

    far = shift(x0, "y", 2)
    xs = [x0, far, shift(x0, "y", 1), shift(x0, "y", 3)]

    weights, sums = call(
        prep_kernel,
        (jax.ShapeDtypeStruct((FD, 2 * FB), bf16), jax.ShapeDtypeStruct((8, 2 * FB), f32)),
        2, 24, 2 * 8 * FD * 2 * FB, 4 * FD * 2 * FB, name="prep",
    )(where, own, swap(own, "core"))
    products = call(
        project_kernel,
        jax.ShapeDtypeStruct((8, TB + EXTRA, FB), bf16),
        6, 40, 2 * 4 * TB * FD * 2 * FB, 6 << 20, name="project",
        scratch=(pltpu.VMEM((4, TB, FD), bf16),),
    )(where, *xs, weights, sums)
    received = lax.all_to_all(products, ("core",) + REDUCE, split_axis=0, concat_axis=0, tiled=True)
    q, kv = call(
        norm_kernel,
        (jax.ShapeDtypeStruct((2 * TB, HS), bf16), jax.ShapeDtypeStruct((4, 2 * TB, 2 * HS), bf16)),
        3, 24, 10 * 8 * TB * FB, 2 << 20, name="norm",
    )(where, received, q_gain, k_gain)

    qs = [q] + [swap(q, GATHER, k, 4) for k in (1, 2, 3)]
    kvs = lax.all_to_all(kv, REDUCE, split_axis=0, concat_axis=0, tiled=True)
    partial = call(
        attend_kernel,
        jax.ShapeDtypeStruct((4, HS + EXTRA, 2 * TB), bf16),
        5, 40, 4 * 1024 * 1024 * HS, 2 << 20, 1 << 20, name="attend",
        scratch=(pltpu.VMEM((4, 2 * TB, HS), bf16),),
    )(where, *qs, kvs)
    gathered = lax.all_to_all(partial, GATHER, split_axis=0, concat_axis=0, tiled=True)
    out = call(
        combine_kernel,
        jax.ShapeDtypeStruct((2 * TB, HS), f32),
        1, 16, 8 * HS * 2 * TB, 1 << 20, name="combine",
    )(where, gathered)
    return out.reshape(2 * TB, 1, HS)


def solution(mesh):
    split = Mesh(mesh.devices.reshape(4, 4, 2, 4, 4), AXES)
    row, col = ("y", "zh", "core"), ("x", "zl")
    return jax.shard_map(
        body,
        mesh=split,
        in_specs=(P(row, col), P(col), P(col, row, None), P(row, None), P(row, None)),
        out_specs=P(col, row, None),
        check_vma=False,
    )
```

```python
import jax
import jax.numpy as jnp
from jax import lax
from jax.experimental import pallas as pl
from jax.experimental.pallas import tpu as pltpu
from jax.sharding import Mesh, PartitionSpec as P

D = 6144
HS = 128
FB = 384
FD = 4 * FB
TB = 128
QT = 32
EXTRA = 16
EPS = 1e-06

bf16 = jnp.bfloat16
f32 = jnp.float32

AXES = ("y", "zh", "core", "xa", "xb", "zg", "zr")
GATHER = ("xb", "zg")
REDUCE = ("xa", "zr")


def pieces(v):
    a = v.astype(bf16)
    r = v - a.astype(f32)
    b = r.astype(bf16)
    c = (r - b.astype(f32)).astype(bf16)
    return a.astype(f32), b.astype(f32), c.astype(f32)


def shift(x, axis, k):
    return lax.ppermute(x, axis, [(i, (i + k) % 4) for i in range(4)])


def swap(x, axis, k=1, n=2):
    return lax.ppermute(x, axis, [(i, i ^ k) for i in range(n)])


def call(kernel, out_shape, n_vmem, limit, flops, nbytes, trans=0, name=None, scratch=()):
    return pl.pallas_call(
        kernel,
        out_shape=out_shape,
        in_specs=[pl.BlockSpec(memory_space=pltpu.SMEM)] + [pl.BlockSpec(memory_space=pltpu.VMEM)] * n_vmem,
        scratch_shapes=scratch,
        out_specs=jax.tree.map(lambda _: pl.BlockSpec(memory_space=pltpu.VMEM), out_shape),
        compiler_params=pltpu.CompilerParams(vmem_limit_bytes=limit << 20),
        cost_estimate=pl.CostEstimate(flops=flops, bytes_accessed=nbytes, transcendentals=trans),
        name=name,
    )


def pair_kernel(s_ref, a_ref, b_ref, out_ref):
    out_ref[0] = a_ref[...]
    out_ref[1] = b_ref[...]


def prep_kernel(s_ref, own_ref, oth_ref, w_ref, sums_ref):
    core = s_ref[0]
    for b in range(4):
        j = s_ref[4 + b]
        own, oth = own_ref[j], oth_ref[j]
        w_ref[b * FB : (b + 1) * FB, 0:FB] = jnp.where(core == 0, own, oth)
        w_ref[b * FB : (b + 1) * FB, FB : 2 * FB] = jnp.where(core == 0, oth, own)
    sums_ref[...] = jnp.dot(jnp.ones((8, FD), bf16), w_ref[...], preferred_element_type=f32)


def project_kernel(s_ref, xa_ref, xb_ref, w_ref, sums_ref, *refs):
    *before, out_ref, stats_ref, xs_ref = refs
    first = 1 if before else 0
    for k, x_ref in ((first, xa_ref), (first + 2, xb_ref)):
        high = lax.rem(s_ref[1] - k + 4, 4) // 2
        for a in range(4):
            to = pl.multiple_of(high * (4 * QT) + a % 2 * (2 * QT) + a // 2 * QT, QT)
            for b in range(4):
                xs_ref[pl.ds(to, QT), b * FB : (b + 1) * FB] = x_ref[a * 4 + b]
    x = xs_ref[...]
    n = x.shape[0]
    total = jnp.zeros((n, 128), f32)
    squares = jnp.zeros((n, 128), f32)
    for i in range(FD // 128):
        t = x[:, i * 128 : (i + 1) * 128].astype(f32)
        total = total + t
        squares = squares + t * t
    ones = jnp.ones((8, 128), f32)
    nt = (((1,), (1,)), ((), ()))
    s1 = lax.dot_general(ones, total, nt, precision=lax.Precision.HIGHEST, preferred_element_type=f32)
    s2 = lax.dot_general(ones, squares, nt, precision=lax.Precision.HIGHEST, preferred_element_type=f32)
    stats = jnp.concatenate([s1[0:1], s2[0:1], jnp.zeros((6, n), f32)], axis=0)
    stats_ref[...] = stats
    mean = jnp.sum(total, axis=1, keepdims=True) * (1.0 / FD)
    colsum = sums_ref[0:1, :]
    prod = (jnp.dot(x, w_ref[...], preferred_element_type=f32) - mean * colsum).astype(bf16)
    rows = 2 * QT
    for a in range(4):
        for h in range(2):
            out_ref[h * 4 + a, 0:rows, :] = prod[a * rows : (a + 1) * rows, h * FB : (h + 1) * FB]
    if before:
        col_rows = jnp.concatenate(pieces(colsum), axis=0)
        for a in range(4):
            at = slice(a * rows, (a + 1) * rows)
            both = jnp.concatenate([before[0][:, at], stats[:, at]], axis=1)
            rest = jnp.concatenate(pieces(both[0:1]) + pieces(both[1:2]), axis=0)
            rest = jnp.concatenate([rest, jnp.zeros((6, FB - TB), f32)], axis=1)
            for h in range(2):
                out_ref[h * 4 + a, rows : rows + EXTRA, :] = jnp.concatenate(
                    [rest, col_rows[:, h * FB : (h + 1) * FB], jnp.zeros((EXTRA - 9, FB), f32)], axis=0
                ).astype(bf16)


def norm_kernel(s_ref, ra_ref, rb_ref, qg_ref, kg_ref, q_ref, kv_ref):
    for half in range(2):
        s1, s2, cs = [], [], []
        acc = jnp.zeros((TB, 3 * HS), f32)
        for x in range(4):
            blk = half * 4 + x
            acc = acc + jnp.concatenate([ra_ref[blk], rb_ref[blk, 0 : 2 * QT, :]], axis=0).astype(f32)
            e = rb_ref[blk, 2 * QT : 2 * QT + EXTRA, :].astype(f32)
            s1.append(e[0:1, 0:TB] + e[1:2, 0:TB] + e[2:3, 0:TB])
            s2.append(e[3:4, 0:TB] + e[4:5, 0:TB] + e[5:6, 0:TB])
            cs.append(e[6:7] + e[7:8] + e[8:9])
        mean = (s1[0] + s1[1] + s1[2] + s1[3]) * (1.0 / D)
        var = (s2[0] + s2[1] + s2[2] + s2[3]) * (1.0 / D) - mean * mean
        rows = [s * (1.0 / FD) - mean for s in s1] + [lax.rsqrt(var + EPS)]
        cols = jnp.concatenate(rows + [jnp.zeros((TB - 5, TB), f32)], axis=0).T
        for x in range(4):
            acc = acc + cols[:, x : x + 1] * cs[x]
        proj = acc * cols[:, 4:5]

        def head_norm(v, gain):
            c = v - jnp.mean(v, axis=1, keepdims=True)
            return c * lax.rsqrt(jnp.mean(c * c, axis=1, keepdims=True) + EPS) * gain

        at = slice(half * TB, (half + 1) * TB)
        q_ref[at, :] = head_norm(proj[:, 0:HS], qg_ref[...]).astype(bf16)
        keys = head_norm(proj[:, HS : 2 * HS], kg_ref[...]).astype(bf16)
        values = proj[:, 2 * HS : 3 * HS].astype(bf16)
        for x in range(4):
            kv_ref[x, at, 0:HS] = keys
            kv_ref[x, at, HS : 2 * HS] = values


def attend_kernel(s_ref, q0, q1, q2, q3, kv_ref, out_ref, qs_ref):
    for k, q_ref in enumerate((q0, q1, q2, q3)):
        quarter = s_ref[4 + k]
        for a in range(4):
            for half in range(2):
                to = pl.multiple_of(half * TB + quarter * QT, QT)
                qs_ref[a, pl.ds(to, QT), :] = q_ref[half * TB + a * QT : half * TB + (a + 1) * QT, :]
    vts = [kv_ref[c, :, HS : 2 * HS].T for c in range(4)]
    for a in range(4):
        q = qs_ref[a]
        n = q.shape[0]
        total = jnp.zeros((HS, n), f32)
        denom = jnp.zeros((1, n), f32)
        for c in range(4):
            s = lax.dot_general(kv_ref[c, :, 0:HS], q, (((1,), (1,)), ((), ())), preferred_element_type=f32)
            p = jnp.exp(s * (HS ** -0.5))
            denom = denom + jnp.sum(p, axis=0, keepdims=True)
            total = total + jnp.dot(vts[c], p.astype(bf16), preferred_element_type=f32)
        to = lax.rem(s_ref[1] + a // 2, 2) * 2 + a % 2
        out_ref[to, 0:HS, :] = total.astype(bf16)
        out_ref[to, HS : HS + EXTRA, :] = jnp.concatenate(
            pieces(denom) + (jnp.zeros((EXTRA - 3, n), f32),), axis=0
        ).astype(bf16)


def combine_kernel(s_ref, r_ref, out_ref):
    total = jnp.zeros((HS, r_ref.shape[2]), f32)
    denom = jnp.zeros((1, r_ref.shape[2]), f32)
    for j in range(4):
        total = total + r_ref[j, 0:HS, :].astype(f32)
        e = r_ref[j, HS : HS + EXTRA, :].astype(f32)
        denom = denom + (e[0:1] + e[1:2] + e[2:3])
    out_ref[...] = (total * (1.0 / denom)).T


def body(tokens, ln_gain, qkv_weight, q_gain, k_gain):
    y, core, xb, zg = (lax.axis_index(a).astype(jnp.int32) for a in ("y", "core", "xb", "zg"))
    here = xb * 2 + zg
    where = jnp.stack([core, y, xb, zg] + [jnp.bitwise_xor(here, k) for k in range(4)])

    x0 = lax.all_to_all(
        jnp.broadcast_to(tokens.reshape(1, 4, QT, FB), (4, 4, QT, FB)).reshape(16, QT, FB),
        ("zh",) + GATHER, split_axis=0, concat_axis=0, tiled=True,
    )
    w = (ln_gain[:, None] * qkv_weight.reshape(FB, 3 * HS).astype(f32)).astype(bf16)
    pair = call(
        pair_kernel, jax.ShapeDtypeStruct((2, FB, 3 * HS), bf16), 2, 16, 10**11, 0, name="pair"
    )(where, w, swap(w, "zg"))
    own = jnp.concatenate([pair, swap(pair, "xb")], axis=0)

    far = shift(x0, "y", 2)
    xs = [x0, far, shift(x0, "y", 1), shift(x0, "y", 3)]

    own, _ = lax.optimization_barrier((own, x0))
    weights, sums = call(
        prep_kernel,
        (jax.ShapeDtypeStruct((FD, 2 * FB), bf16), jax.ShapeDtypeStruct((8, 2 * FB), f32)),
        2, 24, 0, 0, name="prep",
    )(where, own, swap(own, "core"))
    def project(xa, xb, extra, *before):
        return call(
            project_kernel,
            (jax.ShapeDtypeStruct((8, 2 * QT + extra, FB), bf16), jax.ShapeDtypeStruct((8, 8 * QT), f32)),
            4 + len(before), 40, 10**11 if before else 0, 0, name="project",
            scratch=(pltpu.VMEM((8 * QT, FD), bf16),),
        )(where, xa, xb, weights, sums, *before)

    first, stats = project(xs[0], xs[1], 0)
    second, _ = project(xs[2], xs[3], EXTRA, stats)
    received = [
        lax.all_to_all(p, ("core",) + REDUCE, split_axis=0, concat_axis=0, tiled=True) for p in (first, second)
    ]
    q, kv = call(
        norm_kernel,
        (jax.ShapeDtypeStruct((2 * TB, HS), bf16), jax.ShapeDtypeStruct((4, 2 * TB, 2 * HS), bf16)),
        4, 24, 10 * 8 * TB * FB, 2 << 20, name="norm",
    )(where, *received, q_gain, k_gain)

    qs = [q] + [swap(q, GATHER, k, 4) for k in (1, 2, 3)]
    kvs = lax.all_to_all(kv, REDUCE, split_axis=0, concat_axis=0, tiled=True)
    partial = call(
        attend_kernel,
        jax.ShapeDtypeStruct((4, HS + EXTRA, 2 * TB), bf16),
        5, 40, 4 * 1024 * 1024 * HS, 2 << 20, 1 << 20, name="attend",
        scratch=(pltpu.VMEM((4, 2 * TB, HS), bf16),),
    )(where, *qs, kvs)
    gathered = lax.all_to_all(partial, GATHER, split_axis=0, concat_axis=0, tiled=True)
    out = call(
        combine_kernel,
        jax.ShapeDtypeStruct((2 * TB, HS), f32),
        1, 16, 8 * HS * 2 * TB, 1 << 20, name="combine",
    )(where, gathered)
    return out.reshape(2 * TB, 1, HS)


def solution(mesh):
    split = Mesh(mesh.devices.reshape(4, 4, 2, 2, 2, 2, 2), AXES)
    row, col = ("y", "zh", "core"), ("xa", "xb", "zg", "zr")
    return jax.shard_map(
        body,
        mesh=split,
        in_specs=(P(row, col), P(col), P(col, row, None), P(row, None), P(row, None)),
        out_specs=P(col, row, None),
        check_vma=False,
    )
```

```python
import jax
import jax.numpy as jnp
from jax import lax
from jax.experimental import pallas as pl
from jax.experimental.pallas import tpu as pltpu
from jax.sharding import Mesh, PartitionSpec as P

D = 6144
HS = 128
FB = 384
FD = 4 * FB
TB = 128
QT = 32
EXTRA = 16
EPS = 1e-06
LOG2E = 1.4426950408889634

bf16 = jnp.bfloat16
f32 = jnp.float32

AXES = ("y", "zh", "core", "xa", "xb", "zg", "zr")
GATHER = ("xb", "zg")
REDUCE = ("xa", "zr")


def pieces(v):
    a = v.astype(bf16)
    r = v - a.astype(f32)
    b = r.astype(bf16)
    c = (r - b.astype(f32)).astype(bf16)
    return a.astype(f32), b.astype(f32), c.astype(f32)


def shift(x, axis, k):
    return lax.ppermute(x, axis, [(i, (i + k) % 4) for i in range(4)])


def swap(x, axis, k=1, n=2):
    return lax.ppermute(x, axis, [(i, i ^ k) for i in range(n)])


def call(kernel, out_shape, n_vmem, limit, flops, nbytes, trans=0, name=None, scratch=()):
    return pl.pallas_call(
        kernel,
        out_shape=out_shape,
        in_specs=[pl.BlockSpec(memory_space=pltpu.SMEM)] + [pl.BlockSpec(memory_space=pltpu.VMEM)] * n_vmem,
        scratch_shapes=scratch,
        out_specs=jax.tree.map(lambda _: pl.BlockSpec(memory_space=pltpu.VMEM), out_shape),
        compiler_params=pltpu.CompilerParams(vmem_limit_bytes=limit << 20),
        cost_estimate=pl.CostEstimate(flops=flops, bytes_accessed=nbytes, transcendentals=trans),
        name=name,
    )


def copy_kernel(s_ref, x_ref, out_ref):
    out_ref[...] = x_ref[...]


def prep_kernel(s_ref, *refs):
    own_refs, other_refs, (w_ref, sums_ref) = refs[:4], refs[4:8], refs[8:]
    core = s_ref[0]
    for j in range(4):
        to = pl.multiple_of(s_ref[4 + j] * FB, FB)
        own, oth = own_refs[j][...], other_refs[j][...]
        w_ref[pl.ds(to, FB), 0:FB] = jnp.where(core == 0, own, oth)
        w_ref[pl.ds(to, FB), FB : 2 * FB] = jnp.where(core == 0, oth, own)
    sums_ref[...] = jnp.dot(jnp.ones((8, FD), bf16), w_ref[...], preferred_element_type=f32)


def project_kernel(s_ref, xa_ref, xb_ref, w_ref, sums_ref, *refs):
    *before, out_ref, stats_ref, xs_ref = refs
    first = 1 if before else 0
    for k, x_ref in ((first, xa_ref), (first + 2, xb_ref)):
        high = lax.rem(s_ref[1] - k + 4, 4) // 2
        for a in range(4):
            to = pl.multiple_of(high * (4 * QT) + a % 2 * (2 * QT) + a // 2 * QT, QT)
            for b in range(4):
                xs_ref[pl.ds(to, QT), b * FB : (b + 1) * FB] = x_ref[a * 4 + b]
    x = xs_ref[...]
    n = x.shape[0]
    total = jnp.zeros((n, 128), f32)
    squares = jnp.zeros((n, 128), f32)
    for i in range(FD // 128):
        t = x[:, i * 128 : (i + 1) * 128].astype(f32)
        total = total + t
        squares = squares + t * t
    ones = jnp.ones((8, 128), f32)
    nt = (((1,), (1,)), ((), ()))
    sums = lax.dot_general(
        ones, jnp.concatenate([total, squares], axis=0), nt, precision=lax.Precision.HIGHEST, preferred_element_type=f32
    )
    stats = jnp.concatenate([sums[0:1, 0:n], sums[0:1, n:], jnp.zeros((6, n), f32)], axis=0)
    stats_ref[...] = stats
    mean = jnp.sum(total, axis=1, keepdims=True) * (1.0 / FD)
    colsum = sums_ref[0:1, :]
    prod = (jnp.dot(x, w_ref[...], preferred_element_type=f32) - mean * colsum).astype(bf16)
    rows = 2 * QT
    at0 = first * rows
    for a in range(4):
        for h in range(2):
            out_ref[h * 4 + a, at0 : at0 + rows, :] = prod[a * rows : (a + 1) * rows, h * FB : (h + 1) * FB]
    if before:
        for blk in range(8):
            out_ref[blk, 0:rows, :] = before[1][blk]
        col_rows = jnp.concatenate(pieces(colsum), axis=0)
        for a in range(4):
            at = slice(a * rows, (a + 1) * rows)
            both = jnp.concatenate([before[0][:, at], stats[:, at]], axis=1)
            rest = jnp.concatenate(pieces(both[0:1]) + pieces(both[1:2]), axis=0)
            rest = jnp.concatenate([rest, jnp.zeros((6, FB - TB), f32)], axis=1)
            for h in range(2):
                out_ref[h * 4 + a, 2 * rows : 2 * rows + EXTRA, :] = jnp.concatenate(
                    [rest, col_rows[:, h * FB : (h + 1) * FB], jnp.zeros((EXTRA - 9, FB), f32)], axis=0
                ).astype(bf16)


def norm_kernel(s_ref, r_ref, qg_ref, kg_ref, q_ref, kv_ref):
    for half in range(2):
        s1, s2, cs = [], [], []
        acc = jnp.zeros((TB, 3 * HS), f32)
        for x in range(4):
            blk = half * 4 + x
            acc = acc + r_ref[blk, 0:TB, :].astype(f32)
            e = r_ref[blk, TB : TB + EXTRA, :].astype(f32)
            s1.append(e[0:1, 0:TB] + e[1:2, 0:TB] + e[2:3, 0:TB])
            s2.append(e[3:4, 0:TB] + e[4:5, 0:TB] + e[5:6, 0:TB])
            cs.append(e[6:7] + e[7:8] + e[8:9])
        mean = (s1[0] + s1[1] + s1[2] + s1[3]) * (1.0 / D)
        var = (s2[0] + s2[1] + s2[2] + s2[3]) * (1.0 / D) - mean * mean
        rows = [s * (1.0 / FD) - mean for s in s1] + [lax.rsqrt(var + EPS)]
        cols = jnp.concatenate(rows + [jnp.zeros((TB - 5, TB), f32)], axis=0).T
        for x in range(4):
            acc = acc + cols[:, x : x + 1] * cs[x]
        proj = acc * cols[:, 4:5]

        def head_norm(v, gain):
            c = v - jnp.mean(v, axis=1, keepdims=True)
            return c * lax.rsqrt(jnp.mean(c * c, axis=1, keepdims=True) + EPS) * gain

        at = slice(half * TB, (half + 1) * TB)
        q_ref[at, :] = head_norm(proj[:, 0:HS], qg_ref[...]).astype(bf16)
        keys = head_norm(proj[:, HS : 2 * HS], kg_ref[...]).astype(bf16)
        values = proj[:, 2 * HS : 3 * HS].astype(bf16)
        for x in range(4):
            kv_ref[x, at, 0:HS] = keys
            kv_ref[x, at, HS : 2 * HS] = values


def attend_kernel(s_ref, q0, q1, q2, q3, kv_ref, out_ref, qs_ref):
    for k, q_ref in enumerate((q0, q1, q2, q3)):
        quarter = s_ref[4 + k]
        for a in range(4):
            for half in range(2):
                to = pl.multiple_of(half * TB + quarter * QT, QT)
                qs_ref[a, pl.ds(to, QT), :] = q_ref[half * TB + a * QT : half * TB + (a + 1) * QT, :]
    vts = [kv_ref[c, :, HS : 2 * HS].T for c in range(4)]
    for a in range(4):
        q = qs_ref[a]
        n = q.shape[0]
        total = jnp.zeros((HS, n), f32)
        denom = jnp.zeros((1, n), f32)
        for c in range(4):
            s = lax.dot_general(kv_ref[c, :, 0:HS], q, (((1,), (1,)), ((), ())), preferred_element_type=f32)
            p = jnp.exp2(s * (HS ** -0.5 * LOG2E))
            denom = denom + jnp.sum(p, axis=0, keepdims=True)
            total = total + jnp.dot(vts[c], p.astype(bf16), preferred_element_type=f32)
        to = lax.rem(s_ref[1] + a // 2, 2) * 2 + a % 2
        out_ref[to, 0:HS, :] = total.astype(bf16)
        out_ref[to, HS : HS + EXTRA, :] = jnp.concatenate(
            pieces(denom) + (jnp.zeros((EXTRA - 3, n), f32),), axis=0
        ).astype(bf16)


def combine_kernel(s_ref, r_ref, out_ref):
    total = jnp.zeros((HS, r_ref.shape[2]), f32)
    denom = jnp.zeros((1, r_ref.shape[2]), f32)
    for j in range(4):
        total = total + r_ref[j, 0:HS, :].astype(f32)
        e = r_ref[j, HS : HS + EXTRA, :].astype(f32)
        denom = denom + (e[0:1] + e[1:2] + e[2:3])
    out_ref[...] = (total * (1.0 / denom)).T


def body(tokens, ln_gain, qkv_weight, q_gain, k_gain):
    y, core, xb, zg = (lax.axis_index(a).astype(jnp.int32) for a in ("y", "core", "xb", "zg"))
    here = xb * 2 + zg
    where = jnp.stack([core, y, xb, zg] + [jnp.bitwise_xor(here, k) for k in range(4)])

    x0 = lax.all_to_all(
        jnp.broadcast_to(tokens.reshape(1, 4, QT, FB), (4, 4, QT, FB)).reshape(16, QT, FB),
        ("zh",) + GATHER, split_axis=0, concat_axis=0, tiled=True,
    )
    w = (ln_gain[:, None] * qkv_weight.reshape(FB, 3 * HS).astype(f32)).astype(bf16)
    near = call(
        copy_kernel, jax.ShapeDtypeStruct((FB, 3 * HS), bf16), 1, 16, 10**11, 0, name="copy"
    )(where, swap(w, "zg"))
    w, near = lax.optimization_barrier((w, near))
    own = [w, near, swap(w, "xb"), swap(near, "xb")]

    far = shift(x0, "y", 2)
    xs = [x0, far, shift(x0, "y", 1), shift(x0, "y", 3)]

    weights, sums = call(
        prep_kernel,
        (jax.ShapeDtypeStruct((FD, 2 * FB), bf16), jax.ShapeDtypeStruct((8, 2 * FB), f32)),
        8, 24, 0, 0, name="prep",
    )(where, *own, *[swap(v, "core") for v in own])

    def project(xa, xb, rows, *before):
        return call(
            project_kernel,
            (jax.ShapeDtypeStruct((8, rows, FB), bf16), jax.ShapeDtypeStruct((8, 8 * QT), f32)),
            4 + len(before), 40, 0, 0, name="project",
            scratch=(pltpu.VMEM((8 * QT, FD), bf16),),
        )(where, xa, xb, weights, sums, *before)

    first, stats = project(xs[0], xs[1], 2 * QT)
    second, _ = project(xs[2], xs[3], TB + EXTRA, stats, first)
    received = lax.all_to_all(second, ("core",) + REDUCE, split_axis=0, concat_axis=0, tiled=True)
    q, kv = call(
        norm_kernel,
        (jax.ShapeDtypeStruct((2 * TB, HS), bf16), jax.ShapeDtypeStruct((4, 2 * TB, 2 * HS), bf16)),
        3, 24, 10 * 8 * TB * FB, 2 << 20, name="norm",
    )(where, received, q_gain, k_gain)

    qs = [q] + [swap(q, GATHER, k, 4) for k in (1, 2, 3)]
    kvs = lax.all_to_all(kv, REDUCE, split_axis=0, concat_axis=0, tiled=True)
    partial = call(
        attend_kernel,
        jax.ShapeDtypeStruct((4, HS + EXTRA, 2 * TB), bf16),
        5, 40, 4 * 1024 * 1024 * HS, 2 << 20, 1 << 20, name="attend",
        scratch=(pltpu.VMEM((4, 2 * TB, HS), bf16),),
    )(where, *qs, kvs)
    gathered = lax.all_to_all(partial, GATHER, split_axis=0, concat_axis=0, tiled=True)
    out = call(
        combine_kernel,
        jax.ShapeDtypeStruct((2 * TB, HS), f32),
        1, 16, 8 * HS * 2 * TB, 1 << 20, name="combine",
    )(where, gathered)
    return out.reshape(2 * TB, 1, HS)


def solution(mesh):
    split = Mesh(mesh.devices.reshape(4, 4, 2, 2, 2, 2, 2), AXES)
    row, col = ("y", "zh", "core"), ("xa", "xb", "zg", "zr")
    return jax.shard_map(
        body,
        mesh=split,
        in_specs=(P(row, col), P(col), P(col, row, None), P(row, None), P(row, None)),
        out_specs=P(col, row, None),
        check_vma=False,
    )
```

```python
import jax
import jax.numpy as jnp
from jax import lax
from jax.experimental import pallas as pl
from jax.experimental.pallas import tpu as pltpu
from jax.sharding import Mesh, PartitionSpec as P

D = 6144
HS = 128
FB = 384
FD = 4 * FB
TB = 128
QT = 32
EXTRA = 16
EPS = 1e-06
LOG2E = 1.4426950408889634

bf16 = jnp.bfloat16
f32 = jnp.float32

AXES = ("y", "zh", "core", "xa", "xb", "zg", "zr")
GATHER = ("xb", "zg")
REDUCE = ("xa", "zr")


def pieces(v):
    a = v.astype(bf16)
    r = v - a.astype(f32)
    b = r.astype(bf16)
    c = (r - b.astype(f32)).astype(bf16)
    return a.astype(f32), b.astype(f32), c.astype(f32)


def shift(x, axis, k):
    return lax.ppermute(x, axis, [(i, (i + k) % 4) for i in range(4)])


def swap(x, axis, k=1, n=2):
    return lax.ppermute(x, axis, [(i, i ^ k) for i in range(n)])


def call(kernel, out_shape, n_vmem, limit, flops, nbytes, trans=0, name=None, scratch=()):
    return pl.pallas_call(
        kernel,
        out_shape=out_shape,
        in_specs=[pl.BlockSpec(memory_space=pltpu.SMEM)] + [pl.BlockSpec(memory_space=pltpu.VMEM)] * n_vmem,
        scratch_shapes=scratch,
        out_specs=jax.tree.map(lambda _: pl.BlockSpec(memory_space=pltpu.VMEM), out_shape),
        compiler_params=pltpu.CompilerParams(vmem_limit_bytes=limit << 20),
        cost_estimate=pl.CostEstimate(flops=flops, bytes_accessed=nbytes, transcendentals=trans),
        name=name,
    )


def copy_kernel(s_ref, x_ref, out_ref):
    out_ref[...] = x_ref[...]


def prep_kernel(s_ref, *refs):
    own_refs, other_refs, (w_ref, sums_ref) = refs[:4], refs[4:8], refs[8:]
    core = s_ref[0]
    for j in range(4):
        to = pl.multiple_of(s_ref[4 + j] * FB, FB)
        own, oth = own_refs[j][...], other_refs[j][...]
        w_ref[pl.ds(to, FB), 0:FB] = jnp.where(core == 0, own, oth)
        w_ref[pl.ds(to, FB), FB : 2 * FB] = jnp.where(core == 0, oth, own)
    sums_ref[...] = jnp.dot(jnp.ones((8, FD), bf16), w_ref[...], preferred_element_type=f32)


def project_kernel(s_ref, xa_ref, xb_ref, w_ref, sums_ref, *refs):
    *before, out_ref, stats_ref, xs_ref = refs
    first = 1 if before else 0
    for k, x_ref in ((first, xa_ref), (first + 2, xb_ref)):
        high = lax.rem(s_ref[1] - k + 4, 4) // 2
        for a in range(4):
            to = pl.multiple_of(high * (4 * QT) + a % 2 * (2 * QT) + a // 2 * QT, QT)
            for b in range(4):
                xs_ref[pl.ds(to, QT), b * FB : (b + 1) * FB] = x_ref[a * 4 + b]
    x = xs_ref[...]
    n = x.shape[0]
    total = jnp.zeros((n, 128), f32)
    squares = jnp.zeros((n, 128), f32)
    for i in range(FD // 128):
        t = x[:, i * 128 : (i + 1) * 128].astype(f32)
        total = total + t
        squares = squares + t * t
    ones = jnp.ones((8, 128), f32)
    nt = (((1,), (1,)), ((), ()))
    sums = lax.dot_general(
        ones, jnp.concatenate([total, squares], axis=0), nt, precision=lax.Precision.HIGHEST, preferred_element_type=f32
    )
    stats = jnp.concatenate([sums[0:1, 0:n], sums[0:1, n:], jnp.zeros((6, n), f32)], axis=0)
    stats_ref[...] = stats
    mean = jnp.sum(total, axis=1, keepdims=True) * (1.0 / FD)
    colsum = sums_ref[0:1, :]
    prod = (jnp.dot(x, w_ref[...], preferred_element_type=f32) - mean * colsum).astype(bf16)
    rows = 2 * QT
    at0 = first * rows
    for a in range(4):
        for h in range(2):
            out_ref[h * 4 + a, at0 : at0 + rows, :] = prod[a * rows : (a + 1) * rows, h * FB : (h + 1) * FB]
    if before:
        for blk in range(8):
            out_ref[blk, 0:rows, :] = before[1][blk]
        col_rows = jnp.concatenate(pieces(colsum), axis=0)
        for a in range(4):
            at = slice(a * rows, (a + 1) * rows)
            both = jnp.concatenate([before[0][:, at], stats[:, at]], axis=1)
            rest = jnp.concatenate(pieces(both[0:1]) + pieces(both[1:2]), axis=0)
            rest = jnp.concatenate([rest, jnp.zeros((6, FB - TB), f32)], axis=1)
            for h in range(2):
                out_ref[h * 4 + a, 2 * rows : 2 * rows + EXTRA, :] = jnp.concatenate(
                    [rest, col_rows[:, h * FB : (h + 1) * FB], jnp.zeros((EXTRA - 9, FB), f32)], axis=0
                ).astype(bf16)


def norm_kernel(s_ref, r_ref, qg_ref, kg_ref, q_ref, kv_ref):
    s1, s2, cs = [], [], []
    acc = jnp.zeros((2 * TB, 3 * HS), f32)
    for x in range(4):
        acc = acc + jnp.concatenate([r_ref[x, 0:TB, :], r_ref[4 + x, 0:TB, :]], axis=0).astype(f32)
        e0, e1 = (r_ref[b, TB : TB + EXTRA, :].astype(f32) for b in (x, 4 + x))
        e = jnp.concatenate([e0[:, 0:TB], e1[:, 0:TB]], axis=1)
        s1.append(e[0:1] + e[1:2] + e[2:3])
        s2.append(e[3:4] + e[4:5] + e[5:6])
        cs.append(e0[6:7] + e0[7:8] + e0[8:9])
    mean = (s1[0] + s1[1] + s1[2] + s1[3]) * (1.0 / D)
    var = (s2[0] + s2[1] + s2[2] + s2[3]) * (1.0 / D) - mean * mean
    rows = [s * (1.0 / FD) - mean for s in s1] + [lax.rsqrt(var + EPS)]
    cols = jnp.concatenate(rows + [jnp.zeros((TB - 5, 2 * TB), f32)], axis=0).T
    for x in range(4):
        acc = acc + cols[:, x : x + 1] * cs[x]
    proj = acc * cols[:, 4:5]

    def head_norm(v, gain):
        c = v - jnp.mean(v, axis=1, keepdims=True)
        return c * lax.rsqrt(jnp.mean(c * c, axis=1, keepdims=True) + EPS) * gain

    q_ref[...] = head_norm(proj[:, 0:HS], qg_ref[...]).astype(bf16)
    keys = head_norm(proj[:, HS : 2 * HS], kg_ref[...]).astype(bf16)
    values = proj[:, 2 * HS : 3 * HS].astype(bf16)
    for x in range(4):
        kv_ref[x, :, 0:HS] = keys
        kv_ref[x, :, HS : 2 * HS] = values


def attend_kernel(s_ref, q0, q1, q2, q3, kv_ref, out_ref, qs_ref):
    for k, q_ref in enumerate((q0, q1, q2, q3)):
        quarter = s_ref[4 + k]
        for a in range(4):
            for half in range(2):
                to = pl.multiple_of(half * TB + quarter * QT, QT)
                qs_ref[a, pl.ds(to, QT), :] = q_ref[half * TB + a * QT : half * TB + (a + 1) * QT, :]
    vts = [kv_ref[c, :, HS : 2 * HS].T for c in range(4)]
    for a in range(4):
        q = qs_ref[a]
        n = q.shape[0]
        total = jnp.zeros((HS, n), f32)
        denom = jnp.zeros((1, n), f32)
        for c in range(4):
            s = lax.dot_general(kv_ref[c, :, 0:HS], q, (((1,), (1,)), ((), ())), preferred_element_type=f32)
            p = jnp.exp2(s * (HS ** -0.5 * LOG2E))
            denom = denom + jnp.sum(p, axis=0, keepdims=True)
            total = total + jnp.dot(vts[c], p.astype(bf16), preferred_element_type=f32)
        to = lax.rem(s_ref[1] + a // 2, 2) * 2 + a % 2
        out_ref[to, 0:HS, :] = total.astype(bf16)
        out_ref[to, HS : HS + EXTRA, :] = jnp.concatenate(
            pieces(denom) + (jnp.zeros((EXTRA - 3, n), f32),), axis=0
        ).astype(bf16)


def combine_kernel(s_ref, r_ref, out_ref):
    total = jnp.zeros((HS, r_ref.shape[2]), f32)
    denom = jnp.zeros((1, r_ref.shape[2]), f32)
    for j in range(4):
        total = total + r_ref[j, 0:HS, :].astype(f32)
        e = r_ref[j, HS : HS + EXTRA, :].astype(f32)
        denom = denom + (e[0:1] + e[1:2] + e[2:3])
    out_ref[...] = (total * (1.0 / denom)).T


def body(tokens, ln_gain, qkv_weight, q_gain, k_gain):
    y, core, xb, zg = (lax.axis_index(a).astype(jnp.int32) for a in ("y", "core", "xb", "zg"))
    here = xb * 2 + zg
    where = jnp.stack([core, y, xb, zg] + [jnp.bitwise_xor(here, k) for k in range(4)])

    x0 = lax.all_to_all(
        jnp.broadcast_to(tokens.reshape(1, 4, QT, FB), (4, 4, QT, FB)).reshape(16, QT, FB),
        ("zh",) + GATHER, split_axis=0, concat_axis=0, tiled=True,
    )
    w = (ln_gain[:, None] * qkv_weight.reshape(FB, 3 * HS).astype(f32)).astype(bf16)
    near = call(
        copy_kernel, jax.ShapeDtypeStruct((FB, 3 * HS), bf16), 1, 16, 10**11, 0, name="copy"
    )(where, swap(w, "zg"))
    w, near = lax.optimization_barrier((w, near))
    own = [w, near, swap(w, "xb"), swap(near, "xb")]

    far = shift(x0, "y", 2)
    xs = [x0, far, shift(x0, "y", 1), shift(x0, "y", 3)]

    weights, sums = call(
        prep_kernel,
        (jax.ShapeDtypeStruct((FD, 2 * FB), bf16), jax.ShapeDtypeStruct((8, 2 * FB), f32)),
        8, 24, 0, 0, name="prep",
    )(where, *own, *[swap(v, "core") for v in own])

    def project(xa, xb, rows, *before):
        return call(
            project_kernel,
            (jax.ShapeDtypeStruct((8, rows, FB), bf16), jax.ShapeDtypeStruct((8, 8 * QT), f32)),
            4 + len(before), 40, 0, 0, name="project",
            scratch=(pltpu.VMEM((8 * QT, FD), bf16),),
        )(where, xa, xb, weights, sums, *before)

    first, stats = project(xs[0], xs[1], 2 * QT)
    second, _ = project(xs[2], xs[3], TB + EXTRA, stats, first)
    received = lax.all_to_all(second, ("core",) + REDUCE, split_axis=0, concat_axis=0, tiled=True)
    q, kv = call(
        norm_kernel,
        (jax.ShapeDtypeStruct((2 * TB, HS), bf16), jax.ShapeDtypeStruct((4, 2 * TB, 2 * HS), bf16)),
        3, 24, 10 * 8 * TB * FB, 2 << 20, name="norm",
    )(where, received, q_gain, k_gain)

    qs = [q] + [swap(q, GATHER, k, 4) for k in (1, 2, 3)]
    kvs = lax.all_to_all(kv, REDUCE, split_axis=0, concat_axis=0, tiled=True)
    partial = call(
        attend_kernel,
        jax.ShapeDtypeStruct((4, HS + EXTRA, 2 * TB), bf16),
        5, 40, 4 * 1024 * 1024 * HS, 2 << 20, 1 << 20, name="attend",
        scratch=(pltpu.VMEM((4, 2 * TB, HS), bf16),),
    )(where, *qs, kvs)
    gathered = lax.all_to_all(partial, GATHER, split_axis=0, concat_axis=0, tiled=True)
    out = call(
        combine_kernel,
        jax.ShapeDtypeStruct((2 * TB, HS), f32),
        1, 16, 8 * HS * 2 * TB, 1 << 20, name="combine",
    )(where, gathered)
    return out.reshape(2 * TB, 1, HS)


def solution(mesh):
    split = Mesh(mesh.devices.reshape(4, 4, 2, 2, 2, 2, 2), AXES)
    row, col = ("y", "zh", "core"), ("xa", "xb", "zg", "zr")
    return jax.shard_map(
        body,
        mesh=split,
        in_specs=(P(row, col), P(col), P(col, row, None), P(row, None), P(row, None)),
        out_specs=P(col, row, None),
        check_vma=False,
    )
```

```python
import jax
import jax.numpy as jnp
from jax import lax
from jax.experimental import pallas as pl
from jax.experimental.pallas import tpu as pltpu
from jax.sharding import Mesh, PartitionSpec as P

D = 6144
HS = 128
FB = 384
FD = 4 * FB
TB = 128
QT = 32
EXTRA = 16
EPS = 1e-06
LOG2E = 1.4426950408889634

bf16 = jnp.bfloat16
f32 = jnp.float32

AXES = ("y", "zh", "core", "xa", "xb", "zg", "zr")
GATHER = ("xb", "zg")
REDUCE = ("xa", "zr")


def pieces(v):
    a = v.astype(bf16)
    r = v - a.astype(f32)
    b = r.astype(bf16)
    c = (r - b.astype(f32)).astype(bf16)
    return a.astype(f32), b.astype(f32), c.astype(f32)


def shift(x, axis, k):
    return lax.ppermute(x, axis, [(i, (i + k) % 4) for i in range(4)])


def swap(x, axis, k=1, n=2):
    return lax.ppermute(x, axis, [(i, i ^ k) for i in range(n)])


def call(kernel, out_shape, n_vmem, limit, flops, nbytes, trans=0, name=None, scratch=()):
    return pl.pallas_call(
        kernel,
        out_shape=out_shape,
        in_specs=[pl.BlockSpec(memory_space=pltpu.SMEM)] + [pl.BlockSpec(memory_space=pltpu.VMEM)] * n_vmem,
        scratch_shapes=scratch,
        out_specs=jax.tree.map(lambda _: pl.BlockSpec(memory_space=pltpu.VMEM), out_shape),
        compiler_params=pltpu.CompilerParams(vmem_limit_bytes=limit << 20),
        cost_estimate=pl.CostEstimate(flops=flops, bytes_accessed=nbytes, transcendentals=trans),
        name=name,
    )


def repeat_kernel(x_ref, out_ref, sems):
    copies = [pltpu.make_async_copy(x_ref, out_ref.at[a], sems.at[a]) for a in range(4)]
    for c in copies:
        c.start()
    for c in copies:
        c.wait()


def repeat(x):
    return pl.pallas_call(
        repeat_kernel,
        out_shape=jax.ShapeDtypeStruct((4,) + x.shape, x.dtype),
        in_specs=[pl.BlockSpec(memory_space=pl.ANY)],
        out_specs=pl.BlockSpec(memory_space=pl.ANY),
        scratch_shapes=[pltpu.SemaphoreType.DMA((4,))],
        compiler_params=pltpu.CompilerParams(vmem_limit_bytes=8 << 20),
        cost_estimate=pl.CostEstimate(flops=0, bytes_accessed=1 << 19, transcendentals=0),
        name="repeat",
    )(x)


def copy_kernel(s_ref, x_ref, out_ref):
    out_ref[...] = x_ref[...]


def prep_kernel(s_ref, *refs):
    own_refs, other_refs, (w_ref, sums_ref) = refs[:4], refs[4:8], refs[8:]
    core = s_ref[0]
    for j in range(4):
        to = pl.multiple_of(s_ref[4 + j] * FB, FB)
        own, oth = own_refs[j][...], other_refs[j][...]
        w_ref[pl.ds(to, FB), 0:FB] = jnp.where(core == 0, own, oth)
        w_ref[pl.ds(to, FB), FB : 2 * FB] = jnp.where(core == 0, oth, own)
    sums_ref[...] = jnp.dot(jnp.ones((8, FD), bf16), w_ref[...], preferred_element_type=f32)


def project_kernel(s_ref, xa_ref, xb_ref, w_ref, sums_ref, *refs):
    *before, out_ref, stats_ref, xs_ref = refs
    first = 1 if before else 0
    for k, x_ref in ((first, xa_ref), (first + 2, xb_ref)):
        high = lax.rem(s_ref[1] - k + 4, 4) // 2
        for a in range(4):
            to = pl.multiple_of(high * (4 * QT) + a % 2 * (2 * QT) + a // 2 * QT, QT)
            for b in range(4):
                xs_ref[pl.ds(to, QT), b * FB : (b + 1) * FB] = x_ref[a * 4 + b]
    x = xs_ref[...]
    n = x.shape[0]
    total = jnp.zeros((n, 128), f32)
    squares = jnp.zeros((n, 128), f32)
    for i in range(FD // 128):
        t = x[:, i * 128 : (i + 1) * 128].astype(f32)
        total = total + t
        squares = squares + t * t
    ones = jnp.ones((8, 128), f32)
    nt = (((1,), (1,)), ((), ()))
    sums = lax.dot_general(
        ones, jnp.concatenate([total, squares], axis=0), nt, precision=lax.Precision.HIGHEST, preferred_element_type=f32
    )
    stats = jnp.concatenate([sums[0:1, 0:n], sums[0:1, n:], jnp.zeros((6, n), f32)], axis=0)
    stats_ref[...] = stats
    mean = jnp.sum(total, axis=1, keepdims=True) * (1.0 / FD)
    colsum = sums_ref[0:1, :]
    prod = (jnp.dot(x, w_ref[...], preferred_element_type=f32) - mean * colsum).astype(bf16)
    rows = 2 * QT
    at0 = first * rows
    for a in range(4):
        for h in range(2):
            out_ref[h * 4 + a, at0 : at0 + rows, :] = prod[a * rows : (a + 1) * rows, h * FB : (h + 1) * FB]
    if before:
        for blk in range(8):
            out_ref[blk, 0:rows, :] = before[1][blk]
        col_rows = jnp.concatenate(pieces(colsum), axis=0)
        for a in range(4):
            at = slice(a * rows, (a + 1) * rows)
            both = jnp.concatenate([before[0][:, at], stats[:, at]], axis=1)
            rest = jnp.concatenate(pieces(both[0:1]) + pieces(both[1:2]), axis=0)
            rest = jnp.concatenate([rest, jnp.zeros((6, FB - TB), f32)], axis=1)
            for h in range(2):
                out_ref[h * 4 + a, 2 * rows : 2 * rows + EXTRA, :] = jnp.concatenate(
                    [rest, col_rows[:, h * FB : (h + 1) * FB], jnp.zeros((EXTRA - 9, FB), f32)], axis=0
                ).astype(bf16)


def norm_kernel(s_ref, r_ref, qg_ref, kg_ref, q_ref, kv_ref):
    s1, s2, cs = [], [], []
    acc = jnp.zeros((2 * TB, 3 * HS), f32)
    for x in range(4):
        acc = acc + jnp.concatenate([r_ref[x, 0:TB, :], r_ref[4 + x, 0:TB, :]], axis=0).astype(f32)
        e0, e1 = (r_ref[b, TB : TB + EXTRA, :].astype(f32) for b in (x, 4 + x))
        e = jnp.concatenate([e0[:, 0:TB], e1[:, 0:TB]], axis=1)
        s1.append(e[0:1] + e[1:2] + e[2:3])
        s2.append(e[3:4] + e[4:5] + e[5:6])
        cs.append(e0[6:7] + e0[7:8] + e0[8:9])
    mean = (s1[0] + s1[1] + s1[2] + s1[3]) * (1.0 / D)
    var = (s2[0] + s2[1] + s2[2] + s2[3]) * (1.0 / D) - mean * mean
    rows = [s * (1.0 / FD) - mean for s in s1] + [lax.rsqrt(var + EPS)]
    cols = jnp.concatenate(rows + [jnp.zeros((TB - 5, 2 * TB), f32)], axis=0).T
    for x in range(4):
        acc = acc + cols[:, x : x + 1] * cs[x]
    proj = acc * cols[:, 4:5]

    def head_norm(v, gain):
        c = v - jnp.mean(v, axis=1, keepdims=True)
        return c * lax.rsqrt(jnp.mean(c * c, axis=1, keepdims=True) + EPS) * gain

    q_ref[...] = head_norm(proj[:, 0:HS], qg_ref[...]).astype(bf16)
    keys = head_norm(proj[:, HS : 2 * HS], kg_ref[...]).astype(bf16)
    values = proj[:, 2 * HS : 3 * HS].astype(bf16)
    for x in range(4):
        kv_ref[x, :, 0:HS] = keys
        kv_ref[x, :, HS : 2 * HS] = values


def attend_kernel(s_ref, q0, q1, q2, q3, kv_ref, out_ref, qs_ref):
    for k, q_ref in enumerate((q0, q1, q2, q3)):
        quarter = s_ref[4 + k]
        for a in range(4):
            for half in range(2):
                to = pl.multiple_of(half * TB + quarter * QT, QT)
                qs_ref[a, pl.ds(to, QT), :] = q_ref[half * TB + a * QT : half * TB + (a + 1) * QT, :]
    vts = [kv_ref[c, :, HS : 2 * HS].T for c in range(4)]
    for a in range(4):
        q = qs_ref[a]
        n = q.shape[0]
        total = jnp.zeros((HS, n), f32)
        denom = jnp.zeros((1, n), f32)
        for c in range(4):
            s = lax.dot_general(kv_ref[c, :, 0:HS], q, (((1,), (1,)), ((), ())), preferred_element_type=f32)
            p = jnp.exp2(s * (HS ** -0.5 * LOG2E))
            denom = denom + jnp.sum(p, axis=0, keepdims=True)
            total = total + jnp.dot(vts[c], p.astype(bf16), preferred_element_type=f32)
        to = lax.rem(s_ref[1] + a // 2, 2) * 2 + a % 2
        out_ref[to, 0:HS, :] = total.astype(bf16)
        out_ref[to, HS : HS + EXTRA, :] = jnp.concatenate(
            pieces(denom) + (jnp.zeros((EXTRA - 3, n), f32),), axis=0
        ).astype(bf16)


def combine_kernel(s_ref, r_ref, out_ref):
    total = jnp.zeros((HS, r_ref.shape[2]), f32)
    denom = jnp.zeros((1, r_ref.shape[2]), f32)
    for j in range(4):
        total = total + r_ref[j, 0:HS, :].astype(f32)
        e = r_ref[j, HS : HS + EXTRA, :].astype(f32)
        denom = denom + (e[0:1] + e[1:2] + e[2:3])
    out_ref[...] = (total * (1.0 / denom)).T


def body(tokens, ln_gain, qkv_weight, q_gain, k_gain):
    y, core, xb, zg = (lax.axis_index(a).astype(jnp.int32) for a in ("y", "core", "xb", "zg"))
    here = xb * 2 + zg
    where = jnp.stack([core, y, xb, zg] + [jnp.bitwise_xor(here, k) for k in range(4)])

    x0 = lax.all_to_all(
        repeat(tokens).reshape(16, QT, FB),
        ("zh",) + GATHER, split_axis=0, concat_axis=0, tiled=True,
    )
    w = (ln_gain[:, None] * qkv_weight.reshape(FB, 3 * HS).astype(f32)).astype(bf16)
    near = call(
        copy_kernel, jax.ShapeDtypeStruct((FB, 3 * HS), bf16), 1, 16, 10**11, 0, name="copy"
    )(where, swap(w, "zg"))
    w, near = lax.optimization_barrier((w, near))
    own = [w, near, swap(w, "xb"), swap(near, "xb")]

    far = shift(x0, "y", 2)
    xs = [x0, far, shift(x0, "y", 1), shift(x0, "y", 3)]

    weights, sums = call(
        prep_kernel,
        (jax.ShapeDtypeStruct((FD, 2 * FB), bf16), jax.ShapeDtypeStruct((8, 2 * FB), f32)),
        8, 24, 0, 0, name="prep",
    )(where, *own, *[swap(v, "core") for v in own])

    def project(xa, xb, rows, *before):
        return call(
            project_kernel,
            (jax.ShapeDtypeStruct((8, rows, FB), bf16), jax.ShapeDtypeStruct((8, 8 * QT), f32)),
            4 + len(before), 40, 0, 0, name="project",
            scratch=(pltpu.VMEM((8 * QT, FD), bf16),),
        )(where, xa, xb, weights, sums, *before)

    first, stats = project(xs[0], xs[1], 2 * QT)
    second, _ = project(xs[2], xs[3], TB + EXTRA, stats, first)
    received = lax.all_to_all(second, ("core",) + REDUCE, split_axis=0, concat_axis=0, tiled=True)
    q, kv = call(
        norm_kernel,
        (jax.ShapeDtypeStruct((2 * TB, HS), bf16), jax.ShapeDtypeStruct((4, 2 * TB, 2 * HS), bf16)),
        3, 24, 10 * 8 * TB * FB, 2 << 20, name="norm",
    )(where, received, q_gain, k_gain)

    qs = [q] + [swap(q, GATHER, k, 4) for k in (1, 2, 3)]
    kvs = lax.all_to_all(kv, REDUCE, split_axis=0, concat_axis=0, tiled=True)
    partial = call(
        attend_kernel,
        jax.ShapeDtypeStruct((4, HS + EXTRA, 2 * TB), bf16),
        5, 40, 4 * 1024 * 1024 * HS, 2 << 20, 1 << 20, name="attend",
        scratch=(pltpu.VMEM((4, 2 * TB, HS), bf16),),
    )(where, *qs, kvs)
    gathered = lax.all_to_all(partial, GATHER, split_axis=0, concat_axis=0, tiled=True)
    out = call(
        combine_kernel,
        jax.ShapeDtypeStruct((2 * TB, HS), f32),
        1, 16, 8 * HS * 2 * TB, 1 << 20, name="combine",
    )(where, gathered)
    return out.reshape(2 * TB, 1, HS)


def solution(mesh):
    split = Mesh(mesh.devices.reshape(4, 4, 2, 2, 2, 2, 2), AXES)
    row, col = ("y", "zh", "core"), ("xa", "xb", "zg", "zr")
    return jax.shard_map(
        body,
        mesh=split,
        in_specs=(P(row, col), P(col), P(col, row, None), P(row, None), P(row, None)),
        out_specs=P(col, row, None),
        check_vma=False,
    )
```

```python
import jax
import jax.numpy as jnp
from jax import lax
from jax.experimental import pallas as pl
from jax.experimental.pallas import tpu as pltpu
from jax.sharding import Mesh, PartitionSpec as P

D = 6144
HS = 128
FB = 384
FD = 4 * FB
TB = 128
QT = 32
EXTRA = 16
EPS = 1e-06
LOG2E = 1.4426950408889634

bf16 = jnp.bfloat16
f32 = jnp.float32

AXES = ("y", "zh", "core", "xa", "xb", "zg", "zr")
GATHER = ("xb", "zg")
REDUCE = ("xa", "zr")


def pieces(v):
    a = v.astype(bf16)
    r = v - a.astype(f32)
    b = r.astype(bf16)
    c = (r - b.astype(f32)).astype(bf16)
    return a.astype(f32), b.astype(f32), c.astype(f32)


def shift(x, axis, k):
    return lax.ppermute(x, axis, [(i, (i + k) % 4) for i in range(4)])


def swap(x, axis, k=1, n=2):
    return lax.ppermute(x, axis, [(i, i ^ k) for i in range(n)])


def call(kernel, out_shape, n_vmem, limit, flops, nbytes, trans=0, name=None, scratch=()):
    return pl.pallas_call(
        kernel,
        out_shape=out_shape,
        in_specs=[pl.BlockSpec(memory_space=pltpu.SMEM)] + [pl.BlockSpec(memory_space=pltpu.VMEM)] * n_vmem,
        scratch_shapes=scratch,
        out_specs=jax.tree.map(lambda _: pl.BlockSpec(memory_space=pltpu.VMEM), out_shape),
        compiler_params=pltpu.CompilerParams(vmem_limit_bytes=limit << 20),
        cost_estimate=pl.CostEstimate(flops=flops, bytes_accessed=nbytes, transcendentals=trans),
        name=name,
    )


def copy_kernel(s_ref, x_ref, out_ref):
    out_ref[...] = x_ref[...]


def prep_kernel(s_ref, *refs):
    own_refs, other_refs, (w_ref, sums_ref) = refs[:4], refs[4:8], refs[8:]
    core = s_ref[0]
    for j in range(4):
        to = pl.multiple_of(s_ref[4 + j] * FB, FB)
        own, oth = own_refs[j][...], other_refs[j][...]
        w_ref[pl.ds(to, FB), 0:FB] = jnp.where(core == 0, own, oth)
        w_ref[pl.ds(to, FB), FB : 2 * FB] = jnp.where(core == 0, oth, own)
    sums_ref[...] = jnp.dot(jnp.ones((8, FD), bf16), w_ref[...], preferred_element_type=f32)


def project_kernel(s_ref, xa_ref, xb_ref, w_ref, sums_ref, *refs):
    *before, out_ref, stats_ref, xs_ref = refs
    first = 1 if before else 0
    for k, x_ref in ((first, xa_ref), (first + 2, xb_ref)):
        high = lax.rem(s_ref[1] - k + 4, 4) // 2
        for a in range(4):
            to = pl.multiple_of(high * (4 * QT) + a % 2 * (2 * QT) + a // 2 * QT, QT)
            for b in range(4):
                xs_ref[pl.ds(to, QT), b * FB : (b + 1) * FB] = x_ref[a * 4 + b]
    x = xs_ref[...]
    n = x.shape[0]
    total = jnp.zeros((n, 128), f32)
    squares = jnp.zeros((n, 128), f32)
    for i in range(FD // 128):
        t = x[:, i * 128 : (i + 1) * 128].astype(f32)
        total = total + t
        squares = squares + t * t
    ones = jnp.ones((8, 128), f32)
    nt = (((1,), (1,)), ((), ()))
    sums = lax.dot_general(
        ones, jnp.concatenate([total, squares], axis=0), nt, precision=lax.Precision.HIGHEST, preferred_element_type=f32
    )
    stats = jnp.concatenate([sums[0:1, 0:n], sums[0:1, n:], jnp.zeros((6, n), f32)], axis=0)
    stats_ref[...] = stats
    mean = jnp.sum(total, axis=1, keepdims=True) * (1.0 / FD)
    colsum = sums_ref[0:1, :]
    prod = (jnp.dot(x, w_ref[...], preferred_element_type=f32) - mean * colsum).astype(bf16)
    rows = 2 * QT
    at0 = first * rows
    for a in range(4):
        for h in range(2):
            out_ref[h * 4 + a, at0 : at0 + rows, :] = prod[a * rows : (a + 1) * rows, h * FB : (h + 1) * FB]
    if before:
        for blk in range(8):
            out_ref[blk, 0:rows, :] = before[1][blk]
        col_rows = jnp.concatenate(pieces(colsum), axis=0)
        for a in range(4):
            at = slice(a * rows, (a + 1) * rows)
            both = jnp.concatenate([before[0][:, at], stats[:, at]], axis=1)
            rest = jnp.concatenate(pieces(both[0:1]) + pieces(both[1:2]), axis=0)
            rest = jnp.concatenate([rest, jnp.zeros((6, FB - TB), f32)], axis=1)
            for h in range(2):
                out_ref[h * 4 + a, 2 * rows : 2 * rows + EXTRA, :] = jnp.concatenate(
                    [rest, col_rows[:, h * FB : (h + 1) * FB], jnp.zeros((EXTRA - 9, FB), f32)], axis=0
                ).astype(bf16)


def norm_kernel(s_ref, r_ref, qg_ref, kg_ref, q_ref, kv_ref):
    s1, s2, cs = [], [], []
    acc = jnp.zeros((2 * TB, 3 * HS), f32)
    for x in range(4):
        acc = acc + jnp.concatenate([r_ref[x, 0:TB, :], r_ref[4 + x, 0:TB, :]], axis=0).astype(f32)
        e0, e1 = (r_ref[b, TB : TB + EXTRA, :].astype(f32) for b in (x, 4 + x))
        e = jnp.concatenate([e0[:, 0:TB], e1[:, 0:TB]], axis=1)
        s1.append(e[0:1] + e[1:2] + e[2:3])
        s2.append(e[3:4] + e[4:5] + e[5:6])
        cs.append(e0[6:7] + e0[7:8] + e0[8:9])
    mean = (s1[0] + s1[1] + s1[2] + s1[3]) * (1.0 / D)
    var = (s2[0] + s2[1] + s2[2] + s2[3]) * (1.0 / D) - mean * mean
    rows = [s * (1.0 / FD) - mean for s in s1] + [lax.rsqrt(var + EPS)]
    cols = jnp.concatenate(rows + [jnp.zeros((TB - 5, 2 * TB), f32)], axis=0).T
    for x in range(4):
        acc = acc + cols[:, x : x + 1] * cs[x]
    proj = acc * cols[:, 4:5]

    def head_norm(v, gain):
        c = v - jnp.mean(v, axis=1, keepdims=True)
        return c * lax.rsqrt(jnp.mean(c * c, axis=1, keepdims=True) + EPS) * gain

    q_ref[...] = head_norm(proj[:, 0:HS], qg_ref[...]).astype(bf16)
    keys = head_norm(proj[:, HS : 2 * HS], kg_ref[...]).astype(bf16)
    values = proj[:, 2 * HS : 3 * HS].astype(bf16)
    for x in range(4):
        kv_ref[x, :, 0:HS] = keys
        kv_ref[x, :, HS : 2 * HS] = values


def attend_kernel(s_ref, q0, q3, q1, q2, kv_ref, out_ref, qs_ref):
    for k, q_ref in ((0, q0), (3, q3), (1, q1), (2, q2)):
        quarter = s_ref[4 + k]
        for a in range(4):
            for half in range(2):
                to = pl.multiple_of(half * TB + quarter * QT, QT)
                qs_ref[a, pl.ds(to, QT), :] = q_ref[half * TB + a * QT : half * TB + (a + 1) * QT, :]
    vts = [kv_ref[c, :, HS : 2 * HS].T for c in range(4)]
    for a in range(4):
        q = qs_ref[a]
        n = q.shape[0]
        total = jnp.zeros((HS, n), f32)
        denom = jnp.zeros((1, n), f32)
        for c in range(4):
            s = lax.dot_general(kv_ref[c, :, 0:HS], q, (((1,), (1,)), ((), ())), preferred_element_type=f32)
            p = jnp.exp2(s * (HS ** -0.5 * LOG2E))
            denom = denom + jnp.sum(p, axis=0, keepdims=True)
            total = total + jnp.dot(vts[c], p.astype(bf16), preferred_element_type=f32)
        to = lax.rem(s_ref[1] + a // 2, 2) * 2 + a % 2
        out_ref[to, 0:HS, :] = total.astype(bf16)
        out_ref[to, HS : HS + EXTRA, :] = jnp.concatenate(
            pieces(denom) + (jnp.zeros((EXTRA - 3, n), f32),), axis=0
        ).astype(bf16)


def combine_kernel(s_ref, r_ref, out_ref):
    total = jnp.zeros((HS, r_ref.shape[2]), f32)
    denom = jnp.zeros((1, r_ref.shape[2]), f32)
    for j in range(4):
        total = total + r_ref[j, 0:HS, :].astype(f32)
        e = r_ref[j, HS : HS + EXTRA, :].astype(f32)
        denom = denom + (e[0:1] + e[1:2] + e[2:3])
    out_ref[...] = (total * (1.0 / denom)).T


def body(tokens, ln_gain, qkv_weight, q_gain, k_gain):
    y, core, xb, zg = (lax.axis_index(a).astype(jnp.int32) for a in ("y", "core", "xb", "zg"))
    here = xb * 2 + zg
    where = jnp.stack([core, y, xb, zg] + [jnp.bitwise_xor(here, k) for k in range(4)])

    x0 = lax.all_to_all(
        jnp.broadcast_to(tokens.reshape(1, 4, QT, FB), (4, 4, QT, FB)).reshape(16, QT, FB),
        ("zh",) + GATHER, split_axis=0, concat_axis=0, tiled=True,
    )
    w = (ln_gain[:, None] * qkv_weight.reshape(FB, 3 * HS).astype(f32)).astype(bf16)
    near = call(
        copy_kernel, jax.ShapeDtypeStruct((FB, 3 * HS), bf16), 1, 16, 10**11, 0, name="copy"
    )(where, swap(w, "zg"))
    w, near = lax.optimization_barrier((w, near))
    own = [w, near, swap(w, "xb"), swap(near, "xb")]

    far = shift(x0, "y", 2)
    xs = [x0, far, shift(x0, "y", 1), shift(x0, "y", 3)]

    weights, sums = call(
        prep_kernel,
        (jax.ShapeDtypeStruct((FD, 2 * FB), bf16), jax.ShapeDtypeStruct((8, 2 * FB), f32)),
        8, 24, 0, 0, name="prep",
    )(where, *own, *[swap(v, "core") for v in own])

    def project(xa, xb, rows, *before):
        return call(
            project_kernel,
            (jax.ShapeDtypeStruct((8, rows, FB), bf16), jax.ShapeDtypeStruct((8, 8 * QT), f32)),
            4 + len(before), 40, 0, 0, name="project",
            scratch=(pltpu.VMEM((8 * QT, FD), bf16),),
        )(where, xa, xb, weights, sums, *before)

    first, stats = project(xs[0], xs[1], 2 * QT)
    second, _ = project(xs[2], xs[3], TB + EXTRA, stats, first)
    received = lax.all_to_all(second, ("core",) + REDUCE, split_axis=0, concat_axis=0, tiled=True)
    q, kv = call(
        norm_kernel,
        (jax.ShapeDtypeStruct((2 * TB, HS), bf16), jax.ShapeDtypeStruct((4, 2 * TB, 2 * HS), bf16)),
        3, 24, 10 * 8 * TB * FB, 2 << 20, name="norm",
    )(where, received, q_gain, k_gain)

    qs = [q] + [swap(q, GATHER, k, 4) for k in (3, 1, 2)]
    kvs = lax.all_to_all(kv, REDUCE, split_axis=0, concat_axis=0, tiled=True)
    partial = call(
        attend_kernel,
        jax.ShapeDtypeStruct((4, HS + EXTRA, 2 * TB), bf16),
        5, 40, 4 * 1024 * 1024 * HS, 2 << 20, 1 << 20, name="attend",
        scratch=(pltpu.VMEM((4, 2 * TB, HS), bf16),),
    )(where, *qs, kvs)
    gathered = lax.all_to_all(partial, GATHER, split_axis=0, concat_axis=0, tiled=True)
    out = call(
        combine_kernel,
        jax.ShapeDtypeStruct((2 * TB, HS), f32),
        1, 16, 8 * HS * 2 * TB, 1 << 20, name="combine",
    )(where, gathered)
    return out.reshape(2 * TB, 1, HS)


def solution(mesh):
    split = Mesh(mesh.devices.reshape(4, 4, 2, 2, 2, 2, 2), AXES)
    row, col = ("y", "zh", "core"), ("xa", "xb", "zg", "zr")
    return jax.shard_map(
        body,
        mesh=split,
        in_specs=(P(row, col), P(col), P(col, row, None), P(row, None), P(row, None)),
        out_specs=P(col, row, None),
        check_vma=False,
    )
```
